32 devices in a mesh: gx: 4 (over z), gy: 4 (over x, core), gz: 2 (over y).
Axes of the slice: x: 2, y: 2, z: 4, core: 2. Of those that a mesh axis runs over, the one named last changes fastest.
Arguments:
- coefficients: bfloat16 [8, 16, 4, 512, 128], P('gx', 'gy', 'gz'), may hold values from -6 to 6
- level_weights: bfloat16 [4, 2, 2, 512, 512], replicated, may hold values from -0.125 to 0.125
- coupling: bfloat16 [6, 512, 512], replicated, may hold values from -0.109375 to 0.109375
- positions: float32 [3, 262144], P(None, ('gx', 'gy', 'gz')), may hold values from -1 to 1
- block_leaf: int32 [2048], P(('gx', 'gy', 'gz')), may hold values from 0 to 15
- block_count: int32 [2048], P(('gx', 'gy', 'gz')), may hold values from 1 to 128
Outputs:
- samples: bfloat16 [262144, 128], P(('gx', 'gy', 'gz'))
The draws below stay inside these ranges and needn't reach their ends.
Inputs may be any that keep to these rules, and one draw needn't show every extreme that they name: `block_leaf`: each block names one of the 16 leaves of the device that holds the block.
All inputs are finite; a program needn't handle non-finite values.
Results may differ from the reference program's by a relative error of at most 0.015.
Values may be sent and summed in bfloat16 or wider, within the bound.
A program may use at most 128 MiB of HBM per device.

```python
import math
import jax
import jax.numpy as jnp
import numpy as np
from jax import lax

PTS = 8
ROWS = 128
LEVELS = 4
LX = 2
LY = 4
LZ = 2
BLK_DEV = 64
CHEB = 512
COLS = 128
LB = 16
NLX = 8
NLY = 16
NLZ = 4
NBLK = 2048
NSAMP = 262144
N_GX = 4
N_GY = 4
N_GZ = 2


def touch_ends(values, key, least, top_value):
    index_at = [jax.random.randint(jax.random.fold_in(key, axis), (), 0, length) for axis, length in enumerate(values.shape)]
    longest = values.shape.index(max(values.shape))
    next_to = index_at[:longest] + [(index_at[longest] + 1) % values.shape[longest]] + index_at[longest + 1:]
    return values.at[tuple(index_at)].set(least).at[tuple(next_to)].set(top_value)


def level_of(key, shape, split, low, largest):
    level, own = 1.0, jax.random.fold_in(key, 6)
    for dim, blocks in split:
        steps = jnp.exp(jax.random.uniform(jax.random.fold_in(own, dim), (blocks,), jnp.float32, low / len(split), largest / len(split)))
        level = level * jnp.repeat(steps, shape[dim] // blocks).reshape([-1 if axis == dim else 1 for axis in range(len(shape))])
    return level


def rank_table(number_of, skew):
    weights = [(1 << 20) // math.isqrt(grade ** skew) + 1 for grade in range(1, number_of + 1)]
    deviation = 1 + sum(weights) // (1 << 30)
    return np.cumsum(np.array([max(1, weight // deviation) for weight in weights]))


def ranked_ids(stream_key, shape, amount, slope):
    table = rank_table(amount, slope)
    lot = jax.random.randint(jax.random.fold_in(stream_key, 1), shape, 0, int(table[amount - 1]))
    standing = jnp.searchsorted(jnp.asarray(table, jnp.int32), lot, side="right")
    return jax.random.permutation(jax.random.fold_in(stream_key, 2), amount)[standing].astype(jnp.int32)


def centred(stream_key, dims, scale, reach, shards=(), held_as=jnp.bfloat16):
    array = jax.random.normal(stream_key, dims, jnp.float32) * scale
    if len(shards) > 0:
        array = level_of(stream_key, dims, shards, -0.22, 0.18) * array
    return jnp.clip(array, min=-reach, max=reach).astype(held_as)


def setup_inputs(seed: int = 0) -> dict:
    arg_keys = jax.random.split(jax.random.key(seed), 7)
    return {
        "coefficients": centred(arg_keys[0], (NLX, NLY, NLZ, CHEB, COLS), 1.0, 6.0, ((0, 4), (1, 4), (2, 2))),
        "level_weights": centred(arg_keys[1], (LEVELS, 2, 2, CHEB, CHEB), (4 * CHEB) ** -0.5, 0.125),
        "coupling": centred(arg_keys[2], (6, CHEB, CHEB), (6 * CHEB) ** -0.5, 0.109375),
        "positions": jnp.clip(jax.random.uniform(arg_keys[3], (3, NSAMP), jnp.float32, -1.0, 1.0) * level_of(arg_keys[3], (3, NSAMP), ((1, 32),), -0.4, 0.0), -1.0, 1.0),
        "block_leaf": touch_ends(ranked_ids(arg_keys[4], (NBLK,), LB, 2), jax.random.fold_in(arg_keys[4], 3), 0, LB - 1).astype(jnp.int32),
        "block_count": touch_ends(jax.random.randint(arg_keys[5], (NBLK,), 1, ROWS + 1), jax.random.fold_in(arg_keys[5], 1), 1, ROWS).astype(jnp.int32),
    }


def swapped(block):
    half = block.shape[-1] // 2
    return jnp.concatenate([-block[..., half:], block[..., :half]], axis=-1)


def flipped(block, dim, count, bit):
    shape = block.shape
    width = 1 << bit
    inner = shape[dim] // count * width
    grouped = block.reshape(shape[:dim] + (count // (2 * width), 2, inner) + shape[dim + 1:])
    return jnp.flip(grouped, axis=dim + 1).reshape(shape)


def apply_map(weights, block):
    return jnp.einsum("jk,...kc->...jc", weights.astype(jnp.float32), block.astype(jnp.float32))


def mix(block, other, weights):
    total = apply_map(weights[0, 0], block) + apply_map(weights[0, 1], swapped(block))
    total = total + apply_map(weights[1, 0], other) + apply_map(weights[1, 1], swapped(other))
    return total.astype(jnp.bfloat16)


def lagrange(coords, points):
    nodes = jnp.cos(math.pi * (2.0 * jnp.arange(points, dtype=jnp.float32) + 1.0) / (2.0 * points))
    basis = []
    for j in range(points):
        term = jnp.ones_like(coords)
        for m in range(points):
            if m != j:
                term = term * (coords - nodes[m]) / (nodes[j] - nodes[m])
        basis.append(term)
    return jnp.stack(basis, axis=-1)


def sample_weights(coords, points):
    along_x = lagrange(coords[0], points)
    along_y = lagrange(coords[1], points)
    along_z = lagrange(coords[2], points)
    prod = along_x[..., :, None, None] * along_y[..., None, :, None] * along_z[..., None, None, :]
    return prod.reshape(coords.shape[1:] + (points ** 3,)).astype(jnp.bfloat16)


def reference(coefficients, level_weights, coupling, positions, block_leaf, block_count):
    current = coefficients
    plan = ((0, N_GX, 0), (0, N_GX, 1), (1, N_GY, 0), (2, N_GZ, 0))
    for level in range(4):
        dim, count, bit = plan[level]
        other = flipped(current, dim, count, bit)
        current = mix(current, other, level_weights[level])
    padded = jnp.pad(current, ((1, 1), (1, 1), (1, 1), (0, 0), (0, 0)))
    neighbours = (padded[:-2, 1:-1, 1:-1], padded[2:, 1:-1, 1:-1], padded[1:-1, :-2, 1:-1],
                  padded[1:-1, 2:, 1:-1], padded[1:-1, 1:-1, :-2], padded[1:-1, 1:-1, 2:])
    total = current.astype(jnp.float32)
    for index in range(6):
        total = total + apply_map(coupling[index], neighbours[index])
    grid = total.astype(jnp.bfloat16)
    cheb = grid.shape[3]
    cols = grid.shape[4]
    devices = N_GX * N_GY * N_GZ
    per_device = grid.reshape(N_GX, LX, N_GY, LY, N_GZ, LZ, cheb, cols)
    per_device = per_device.transpose(0, 2, 4, 1, 3, 5, 6, 7).reshape(devices, LX * LY * LZ, cheb, cols)
    coords = positions.reshape(3, devices, BLK_DEV, ROWS).transpose(1, 0, 2, 3)
    leaves = block_leaf.reshape(devices, BLK_DEV)
    counts = block_count.reshape(devices, BLK_DEV)

    def one_device(items):
        leaf_grid, coord, leaf, count = items
        weights = sample_weights(coord, PTS)
        blocks = jnp.take(leaf_grid, leaf, axis=0)
        values = jnp.einsum("brk,bkc->brc", weights.astype(jnp.float32), blocks.astype(jnp.float32))
        live = jnp.arange(ROWS, dtype=jnp.int32)[None, :] < count[:, None]
        values = jnp.where(live[:, :, None], values, jnp.float32(0.0))
        return values.reshape(BLK_DEV * ROWS, cols).astype(jnp.bfloat16)

    result = lax.map(one_device, (per_device, coords, leaves, counts))
    return result.reshape(devices * BLK_DEV * ROWS, cols)
```

```python
import functools
import math

import jax
import jax.numpy as jnp
from jax import lax
from jax.experimental import pallas as pl
from jax.experimental.pallas import tpu as pltpu
from jax.sharding import PartitionSpec as P

PTS = 8
ROWS = 128
MESH = pl.DeviceIdType.MESH
NT = (((1,), (1,)), ((), ()))


def flat(value):
    return value.reshape(-1, value.shape[-1])


def grid_kernel(sizes, x_ref, w_hbm, k_hbm, out_ref, w_ref, k_ref, src, xin, mid, got, pad, res,
                w_sem, k_sem, fs_sem, fr_sem, ms_sem, mr_sem, hs_sem, hr_sem, zs_sem, zr_sem, bs_sem, br_sem):
    nx, ny, nz = sizes
    lx, ly, lz = x_ref.shape[:3]
    groups = 2 * nx
    per = x_ref.shape[-1] // 2 // groups
    gx, gy, gz = lax.axis_index("gx"), lax.axis_index("gy"), lax.axis_index("gz")
    bit = lax.rem(gz, 2)
    base = gz - bit
    me = gx * 2 + bit
    wide_x, wide_z = nx * lx, 2 * lz

    def peer(step):
        other = lax.rem(me + step, groups)
        return other, lax.div(other, 2), lax.rem(other, 2)

    def when(cond):
        return pl.when(cond)

    for level in range(4):
        pltpu.make_async_copy(w_hbm.at[level], w_ref.at[level], w_sem.at[level]).start()
    pltpu.make_async_copy(k_hbm, k_ref, k_sem).start()

    barrier = pltpu.get_barrier_semaphore()
    for step in range(1, groups):
        _, px, pz = peer(step)
        pl.semaphore_signal(barrier, inc=1, device_id=(px, gy, base + pz), device_id_type=MESH)

    @when(gy > 0)
    def _():
        pl.semaphore_signal(barrier, inc=1, device_id=(gx, gy - 1, gz), device_id_type=MESH)

    @when(gy < ny - 1)
    def _():
        pl.semaphore_signal(barrier, inc=1, device_id=(gx, gy + 1, gz), device_id_type=MESH)

    if nz > 2:
        @when(gz > 1)
        def _():
            pl.semaphore_signal(barrier, inc=1, device_id=(gx, gy, gz - 2), device_id_type=MESH)

        @when(gz < nz - 2)
        def _():
            pl.semaphore_signal(barrier, inc=1, device_id=(gx, gy, gz + 2), device_id_type=MESH)

    def turn(t):
        y = lax.rem(3 * t, ly)
        for a in range(lx):
            for b in range(lz):
                block = x_ref[a, y, b].astype(jnp.float32).T
                half = block.shape[0] // 2
                for g in range(groups):
                    both = jnp.concatenate(
                        [block[g * per:(g + 1) * per], block[half + g * per:half + (g + 1) * per]], axis=0
                    )
                    src[g, y, a, b] = both.astype(jnp.bfloat16)
        xin[y, pl.ds(gx * lx, lx), pl.ds(bit * lz, lz)] = src[me, y]

    def forward(t, step):
        y = lax.rem(3 * t, ly)
        other, px, pz = peer(step)
        return pltpu.make_async_remote_copy(
            src_ref=src.at[other, y],
            dst_ref=xin.at[y, pl.ds(gx * lx, lx), pl.ds(bit * lz, lz)],
            send_sem=fs_sem.at[step, y],
            recv_sem=fr_sem.at[step, y],
            device_id=(px, gy, base + pz),
            device_id_type=MESH,
        )

    turn(0)
    def one(cond):
        return jnp.where(cond, 1, 0).astype(jnp.int32)

    peers = groups - 1 + one(gy > 0) + one(gy < ny - 1)
    if nz > 2:
        peers = peers + one(gz > 1) + one(gz < nz - 2)
    pl.semaphore_wait(barrier, peers)

    @pl.loop(0, ly)
    def _(t):
        @when(t > 0)
        def _():
            turn(t)
        for step in range(1, groups):
            forward(t, step).start()

    pad[:, 0] = jnp.zeros_like(pad[:, 0])
    pad[:, wide_x + 1] = jnp.zeros_like(pad[:, 0])

    def no_plane(z):
        for y in range(1, ly + 1):
            pad[y, 1:wide_x + 1, z] = jnp.zeros_like(pad[0, 1:wide_x + 1, 0])

    if nz > 2:
        when(gz < 2)(lambda: no_plane(0))
        when(gz >= nz - 2)(lambda: no_plane(wide_z + 1))
    else:
        no_plane(0)
        no_plane(wide_z + 1)

    @when(gy == 0)
    def _():
        pad[0, 1:wide_x + 1] = jnp.zeros_like(pad[0, 1:wide_x + 1])

    @when(gy == ny - 1)
    def _():
        pad[ly + 1, 1:wide_x + 1] = jnp.zeros_like(pad[0, 1:wide_x + 1])

    def mixed(level, own, other):
        shape = own.shape
        a, b = flat(own), flat(other)
        dot = functools.partial(lax.dot_general, dimension_numbers=NT, preferred_element_type=jnp.float32)
        straight = dot(a, w_ref[level, 0, 0]) + dot(b, w_ref[level, 1, 0])
        cross = dot(a, w_ref[level, 0, 1]) + dot(b, w_ref[level, 1, 1])
        straight = straight.reshape(-1, 2, per, shape[-1])
        cross = cross.reshape(-1, 2, per, shape[-1])
        real = straight[:, 0] - cross[:, 1]
        imag = straight[:, 1] + cross[:, 0]
        return jnp.stack([real, imag], axis=1).reshape(shape).astype(jnp.bfloat16)

    def flip(value, dim, width):
        pieces = []
        for at in range(0, value.shape[dim], 2 * width):
            pieces.append(lax.slice_in_dim(value, at + width, at + 2 * width, axis=dim))
            pieces.append(lax.slice_in_dim(value, at, at + width, axis=dim))
        return jnp.concatenate(pieces, axis=dim)

    def to_core(y):
        return pltpu.make_async_remote_copy(
            src_ref=mid.at[y], dst_ref=got.at[y], send_sem=ms_sem.at[y], recv_sem=mr_sem.at[y],
            device_id=(gx, gy + 1 - 2 * lax.rem(gy, 2), gz), device_id_type=MESH,
        )

    inner = (pl.ds(1, wide_x), pl.ds(1, wide_z))

    def halo(up):
        return pltpu.make_async_remote_copy(
            src_ref=pad.at[(ly if up else 1,) + inner],
            dst_ref=pad.at[(0 if up else ly + 1,) + inner],
            send_sem=hs_sem.at[int(up)], recv_sem=hr_sem.at[int(up)],
            device_id=(gx, gy + 1 if up else gy - 1, gz), device_id_type=MESH,
        )

    def halo_z(up):
        rows = pl.ds(1, ly), pl.ds(1, wide_x)
        return pltpu.make_async_remote_copy(
            src_ref=pad.at[rows + (wide_z if up else 1,)],
            dst_ref=pad.at[rows + (0 if up else wide_z + 1,)],
            send_sem=zs_sem.at[int(up)], recv_sem=zr_sem.at[int(up)],
            device_id=(gx, gy, gz + 2 if up else gz - 2), device_id_type=MESH,
        )

    for level in range(4):
        pltpu.make_async_copy(w_hbm.at[level], w_ref.at[level], w_sem.at[level]).wait()

    @pl.loop(0, ly + 1)
    def _(t):
        @when(t < ly)
        def _():
            y = lax.rem(3 * t, ly)
            for step in range(1, groups):
                forward(t, step).wait_recv()
            own = xin[y]
            own = mixed(0, own, flip(own, 0, lx))
            mid[y] = mixed(1, own, flip(own, 0, 2 * lx))
            to_core(y).start()

        @when(t > 0)
        def _():
            y = lax.rem(3 * (t - 1), ly)
            to_core(y).wait_recv()
            own = mixed(2, mid[y], got[y])
            pad[y + 1, 1:wide_x + 1, 1:wide_z + 1] = mixed(3, own, flip(own, 1, lz))

            @when(jnp.logical_and(y == 0, gy > 0))
            def _():
                halo(False).start()

            @when(jnp.logical_and(y == ly - 1, gy < ny - 1))
            def _():
                halo(True).start()

    if nz > 2:
        @when(gz < nz - 2)
        def _():
            halo_z(True).start()

        @when(gz > 1)
        def _():
            halo_z(False).start()

        @when(gz > 1)
        def _():
            halo_z(True).wait_recv()

        @when(gz < nz - 2)
        def _():
            halo_z(False).wait_recv()

    pltpu.make_async_copy(k_hbm, k_ref, k_sem).wait()

    @when(gy < ny - 1)
    def _():
        halo(False).wait_recv()

    @when(gy > 0)
    def _():
        halo(True).wait_recv()

    def back(y, step):
        other, px, pz = peer(step)
        return pltpu.make_async_remote_copy(
            src_ref=res.at[y, pl.ds(px * lx, lx), pl.ds(pz * lz, lz)],
            dst_ref=out_ref.at[me, y],
            send_sem=bs_sem.at[step, y], recv_sem=br_sem.at[step, y],
            device_id=(px, gy, base + pz), device_id_type=MESH,
        )

    @pl.loop(0, ly)
    def _(t):
        y = ly - 1 - t
        xs, zs = pl.ds(1, wide_x), pl.ds(1, wide_z)
        here = pad[y + 1, xs, zs]
        total = flat(here).astype(jnp.float32)
        places = (
            (y + 1, pl.ds(0, wide_x), zs), (y + 1, pl.ds(2, wide_x), zs),
            (y, xs, zs), (y + 2, xs, zs),
            (y + 1, xs, pl.ds(0, wide_z)), (y + 1, xs, pl.ds(2, wide_z)),
        )
        for d, place in enumerate(places):
            total = total + lax.dot_general(flat(pad[place]), k_ref[d], NT, preferred_element_type=jnp.float32)
        res[y] = total.astype(jnp.bfloat16).reshape(here.shape)
        for step in range(1, groups):
            back(y, step).start()
        out_ref[me, y] = res[y, pl.ds(gx * lx, lx), pl.ds(bit * lz, lz)]

    @pl.loop(0, ly)
    def _(t):
        for step in range(1, groups):
            forward(t, step).wait_send()
            back(t, step).wait_send()
            back(t, step).wait_recv()
        to_core(t).wait_send()

    @when(gy > 0)
    def _():
        halo(False).wait_send()

    @when(gy < ny - 1)
    def _():
        halo(True).wait_send()

    if nz > 2:
        @when(gz < nz - 2)
        def _():
            halo_z(True).wait_send()

        @when(gz > 1)
        def _():
            halo_z(False).wait_send()


def grid_of(coefficients, level_weights, coupling, sizes):
    nx, ny, nz = sizes
    lx, ly, lz, cheb, cols = coefficients.shape
    groups = 2 * nx
    rows = cols // groups
    bf = jnp.bfloat16
    plane = (nx * lx, 2 * lz, rows, cheb)
    dma = pltpu.SemaphoreType.DMA
    anywhere = pl.BlockSpec(memory_space=pl.ANY)
    vmem = pl.BlockSpec(memory_space=pltpu.VMEM)
    return pl.pallas_call(
        functools.partial(grid_kernel, sizes),
        out_shape=jax.ShapeDtypeStruct((groups, ly, lx, lz, rows, cheb), bf),
        in_specs=[vmem, anywhere, anywhere],
        out_specs=vmem,
        scratch_shapes=[
            pltpu.VMEM(level_weights.shape, bf),
            pltpu.VMEM(coupling.shape, bf),
            pltpu.VMEM((groups, ly, lx, lz, rows, cheb), bf),
            pltpu.VMEM((ly,) + plane, bf),
            pltpu.VMEM((ly,) + plane, bf),
            pltpu.VMEM((ly,) + plane, bf),
            pltpu.VMEM((ly + 2, nx * lx + 2, 2 * lz + 2, rows, cheb), bf),
            pltpu.VMEM((ly,) + plane, bf),
            dma((4,)), dma,
            dma((groups, ly)), dma((groups, ly)),
            dma((ly,)), dma((ly,)),
            dma((2,)), dma((2,)), dma((2,)), dma((2,)),
            dma((groups, ly)), dma((groups, ly)),
        ],
        compiler_params=pltpu.CompilerParams(
            collective_id=0, has_side_effects=True, vmem_limit_bytes=56 << 20
        ),
    )(coefficients, level_weights, coupling)


def basis_of(coords):
    nodes = [math.cos(math.pi * (2 * j + 1) / (2 * PTS)) for j in range(PTS)]
    diffs = [coords - jnp.float32(node) for node in nodes]
    basis = []
    for j in range(PTS):
        scale = 1.0
        term = None
        for m in range(PTS):
            if m != j:
                scale *= nodes[j] - nodes[m]
                term = diffs[m] if term is None else term * diffs[m]
        basis.append(term * jnp.float32(1.0 / scale))
    return basis


def sample_kernel(leaf_ref, count_ref, pos_ref, grid_ref, out_ref, held):
    groups, ly, lx, lz, rows, cheb = grid_ref.shape
    per = rows // 2
    for a in range(lx):
        for y in range(ly):
            for b in range(lz):
                parts = [grid_ref[g, y, a, b].astype(jnp.float32) for g in range(groups)]
                whole = [part[:per] for part in parts] + [part[per:] for part in parts]
                held[(a * ly + y) * lz + b] = jnp.concatenate(whole, axis=0).astype(jnp.bfloat16)

    @pl.loop(0, leaf_ref.shape[0])
    def _(i):
        start = pl.multiple_of(i * ROWS, ROWS)
        along = [basis_of(pos_ref[d:d + 1, pl.ds(start, ROWS)]) for d in range(3)]
        last = jnp.concatenate(along[2], axis=0)
        tiles = []
        for jx in range(PTS):
            for jy in range(PTS):
                tiles.append((along[0][jx] * along[1][jy]) * last)
        weights = jnp.concatenate(tiles, axis=0).astype(jnp.bfloat16)
        values = jnp.dot(held[leaf_ref[i]], weights, preferred_element_type=jnp.float32)
        values = values.T
        live = lax.broadcasted_iota(jnp.int32, values.shape, 0) < count_ref[i]
        out_ref[pl.ds(start, ROWS), :] = jnp.where(live, values, 0.0).astype(jnp.bfloat16)


def samples_of(grid, positions, block_leaf, block_count):
    groups, ly, lx, lz, rows, cheb = grid.shape
    smem = pl.BlockSpec(memory_space=pltpu.SMEM)
    vmem = pl.BlockSpec(memory_space=pltpu.VMEM)
    return pl.pallas_call(
        sample_kernel,
        out_shape=jax.ShapeDtypeStruct((positions.shape[1], groups * rows), jnp.bfloat16),
        in_specs=[smem, smem, vmem, vmem],
        out_specs=vmem,
        scratch_shapes=[pltpu.VMEM((lx * ly * lz, groups * rows, cheb), jnp.bfloat16)],
        compiler_params=pltpu.CompilerParams(vmem_limit_bytes=40 << 20),
    )(block_leaf, block_count, positions, grid)


def local(sizes, coefficients, level_weights, coupling, positions, block_leaf, block_count):
    grid = grid_of(coefficients, level_weights, coupling, sizes)
    return samples_of(grid, positions, block_leaf, block_count)


def solution(mesh):
    sizes = (mesh.shape["gx"], mesh.shape["gy"], mesh.shape["gz"])
    placed = (
        P("gx", "gy", "gz", None, None),
        P(),
        P(),
        P(None, ("gx", "gy", "gz")),
        P(("gx", "gy", "gz")),
        P(("gx", "gy", "gz")),
    )
    return jax.shard_map(
        functools.partial(local, sizes), mesh=mesh, in_specs=placed,
        out_specs=P(("gx", "gy", "gz"), None), check_vma=False,
    )
```

```python
import functools
import math

import jax
import jax.numpy as jnp
from jax import lax
from jax.experimental import pallas as pl
from jax.experimental.pallas import tpu as pltpu
from jax.sharding import PartitionSpec as P

PTS = 8
ROWS = 128
MESH = pl.DeviceIdType.MESH
NT = (((1,), (1,)), ((), ()))


def flat(value):
    return value.reshape(-1, value.shape[-1])


def basis_of(coords):
    nodes = [math.cos(math.pi * (2 * j + 1) / (2 * PTS)) for j in range(PTS)]
    diffs = [coords - jnp.float32(node) for node in nodes]
    basis = []
    for j in range(PTS):
        scale = 1.0
        term = None
        for m in range(PTS):
            if m != j:
                scale *= nodes[j] - nodes[m]
                term = diffs[m] if term is None else term * diffs[m]
        basis.append(term * jnp.float32(1.0 / scale))
    return basis


def grid_kernel(sizes, leaf_ref, count_ref, x_ref, pos_ref, w_hbm, k_hbm, out_ref,
                w_ref, k_ref, src, xin, mid, got, pad, res, home, held, wts,
                w_sem, k_sem, fs_sem, fr_sem, ms_sem, mr_sem, hs_sem, hr_sem, zs_sem, zr_sem, bs_sem, br_sem):
    nx, ny, nz = sizes
    lx, ly, lz = x_ref.shape[:3]
    groups = 2 * nx
    per = x_ref.shape[-1] // 2 // groups
    gx, gy, gz = lax.axis_index("gx"), lax.axis_index("gy"), lax.axis_index("gz")
    bit = lax.rem(gz, 2)
    base = gz - bit
    me = gx * 2 + bit
    wide_x, wide_z = nx * lx, 2 * lz

    def peer(step):
        other = lax.rem(me + step, groups)
        return other, lax.div(other, 2), lax.rem(other, 2)

    def when(cond):
        return pl.when(cond)

    for level in range(4):
        pltpu.make_async_copy(w_hbm.at[level], w_ref.at[level], w_sem.at[level]).start()
    pltpu.make_async_copy(k_hbm, k_ref, k_sem).start()

    barrier = pltpu.get_barrier_semaphore()
    for step in range(1, groups):
        _, px, pz = peer(step)
        pl.semaphore_signal(barrier, inc=1, device_id=(px, gy, base + pz), device_id_type=MESH)

    @when(gy > 0)
    def _():
        pl.semaphore_signal(barrier, inc=1, device_id=(gx, gy - 1, gz), device_id_type=MESH)

    @when(gy < ny - 1)
    def _():
        pl.semaphore_signal(barrier, inc=1, device_id=(gx, gy + 1, gz), device_id_type=MESH)

    if nz > 2:
        @when(gz > 1)
        def _():
            pl.semaphore_signal(barrier, inc=1, device_id=(gx, gy, gz - 2), device_id_type=MESH)

        @when(gz < nz - 2)
        def _():
            pl.semaphore_signal(barrier, inc=1, device_id=(gx, gy, gz + 2), device_id_type=MESH)

    def turn(t):
        y = lax.rem(ly - t, ly)
        for a in range(lx):
            for b in range(lz):
                block = x_ref[a, y, b].astype(jnp.float32).T
                half = block.shape[0] // 2
                for g in range(groups):
                    both = jnp.concatenate(
                        [block[g * per:(g + 1) * per], block[half + g * per:half + (g + 1) * per]], axis=0
                    )
                    src[g, y, a, b] = both.astype(jnp.bfloat16)
        xin[y, pl.ds(gx * lx, lx), pl.ds(bit * lz, lz)] = src[me, y]

    def forward(t, step):
        y = lax.rem(ly - t, ly)
        other, px, pz = peer(step)
        return pltpu.make_async_remote_copy(
            src_ref=src.at[other, y],
            dst_ref=xin.at[y, pl.ds(gx * lx, lx), pl.ds(bit * lz, lz)],
            send_sem=fs_sem.at[step, y],
            recv_sem=fr_sem.at[step, y],
            device_id=(px, gy, base + pz),
            device_id_type=MESH,
        )

    turn(0)
    def one(cond):
        return jnp.where(cond, 1, 0).astype(jnp.int32)

    peers = groups - 1 + one(gy > 0) + one(gy < ny - 1)
    if nz > 2:
        peers = peers + one(gz > 1) + one(gz < nz - 2)
    pl.semaphore_wait(barrier, peers)

    @pl.loop(0, ly)
    def _(t):
        @when(t > 0)
        def _():
            turn(t)
        for step in range(1, groups):
            forward(t, step).start()

    pad[:, 0] = jnp.zeros_like(pad[:, 0])
    pad[:, wide_x + 1] = jnp.zeros_like(pad[:, 0])

    def no_plane(z):
        for y in range(1, ly + 1):
            pad[y, 1:wide_x + 1, z] = jnp.zeros_like(pad[0, 1:wide_x + 1, 0])

    if nz > 2:
        when(gz < 2)(lambda: no_plane(0))
        when(gz >= nz - 2)(lambda: no_plane(wide_z + 1))
    else:
        no_plane(0)
        no_plane(wide_z + 1)

    @when(gy == 0)
    def _():
        pad[0, 1:wide_x + 1] = jnp.zeros_like(pad[0, 1:wide_x + 1])

    @when(gy == ny - 1)
    def _():
        pad[ly + 1, 1:wide_x + 1] = jnp.zeros_like(pad[0, 1:wide_x + 1])

    def mixed(level, own, other):
        shape = own.shape
        a, b = flat(own), flat(other)
        dot = functools.partial(lax.dot_general, dimension_numbers=NT, preferred_element_type=jnp.float32)
        straight = dot(a, w_ref[level, 0, 0]) + dot(b, w_ref[level, 1, 0])
        cross = dot(a, w_ref[level, 0, 1]) + dot(b, w_ref[level, 1, 1])
        straight = straight.reshape(-1, 2, per, shape[-1])
        cross = cross.reshape(-1, 2, per, shape[-1])
        real = straight[:, 0] - cross[:, 1]
        imag = straight[:, 1] + cross[:, 0]
        return jnp.stack([real, imag], axis=1).reshape(shape).astype(jnp.bfloat16)

    def flip(value, dim, width):
        pieces = []
        for at in range(0, value.shape[dim], 2 * width):
            pieces.append(lax.slice_in_dim(value, at + width, at + 2 * width, axis=dim))
            pieces.append(lax.slice_in_dim(value, at, at + width, axis=dim))
        return jnp.concatenate(pieces, axis=dim)

    def to_core(y):
        return pltpu.make_async_remote_copy(
            src_ref=mid.at[y], dst_ref=got.at[y], send_sem=ms_sem.at[y], recv_sem=mr_sem.at[y],
            device_id=(gx, gy + 1 - 2 * lax.rem(gy, 2), gz), device_id_type=MESH,
        )

    inner = (pl.ds(1, wide_x), pl.ds(1, wide_z))

    def halo(up):
        return pltpu.make_async_remote_copy(
            src_ref=pad.at[(ly if up else 1,) + inner],
            dst_ref=pad.at[(0 if up else ly + 1,) + inner],
            send_sem=hs_sem.at[int(up)], recv_sem=hr_sem.at[int(up)],
            device_id=(gx, gy + 1 if up else gy - 1, gz), device_id_type=MESH,
        )

    def halo_z(up):
        rows = pl.ds(1, ly), pl.ds(1, wide_x)
        return pltpu.make_async_remote_copy(
            src_ref=pad.at[rows + (wide_z if up else 1,)],
            dst_ref=pad.at[rows + (0 if up else wide_z + 1,)],
            send_sem=zs_sem.at[int(up)], recv_sem=zr_sem.at[int(up)],
            device_id=(gx, gy, gz + 2 if up else gz - 2), device_id_type=MESH,
        )

    for level in range(4):
        pltpu.make_async_copy(w_hbm.at[level], w_ref.at[level], w_sem.at[level]).wait()

    def back(y, step):
        other, px, pz = peer(step)
        return pltpu.make_async_remote_copy(
            src_ref=res.at[y, pl.ds(px * lx, lx), pl.ds(pz * lz, lz)],
            dst_ref=home.at[me, y],
            send_sem=bs_sem.at[step, y], recv_sem=br_sem.at[step, y],
            device_id=(px, gy, base + pz), device_id_type=MESH,
        )

    def couple(y):
        xs, zs = pl.ds(1, wide_x), pl.ds(1, wide_z)
        here = pad[y + 1, xs, zs]
        total = flat(here).astype(jnp.float32)
        places = (
            (y + 1, pl.ds(0, wide_x), zs), (y + 1, pl.ds(2, wide_x), zs),
            (y, xs, zs), (y + 2, xs, zs),
            (y + 1, xs, pl.ds(0, wide_z)), (y + 1, xs, pl.ds(2, wide_z)),
        )
        for d, place in enumerate(places):
            total = total + lax.dot_general(flat(pad[place]), k_ref[d], NT, preferred_element_type=jnp.float32)
        res[y] = total.astype(jnp.bfloat16).reshape(here.shape)
        for step in range(1, groups):
            back(y, step).start()
        home[me, y] = res[y, pl.ds(gx * lx, lx), pl.ds(bit * lz, lz)]

    def from_above():
        pltpu.make_async_copy(k_hbm, k_ref, k_sem).wait()

        @when(gy < ny - 1)
        def _():
            halo(False).wait_recv()

    early = nz == 2

    @pl.loop(0, ly + 1)
    def _(t):
        @when(t > 0)
        def _():
            y = lax.rem(ly + 1 - t, ly)
            to_core(y).wait_recv()
            own = mixed(2, mid[y], got[y])
            pad[y + 1, 1:wide_x + 1, 1:wide_z + 1] = mixed(3, own, flip(own, 1, lz))

            @when(jnp.logical_and(y == 0, gy > 0))
            def _():
                halo(False).start()

            @when(jnp.logical_and(y == ly - 1, gy < ny - 1))
            def _():
                halo(True).start()

        if early:
            @when(t == ly - 1)
            def _():
                from_above()
                couple(ly - 1)

        @when(t < ly)
        def _():
            y = lax.rem(ly - t, ly)
            for step in range(1, groups):
                forward(t, step).wait_recv()
            own = xin[y]
            own = mixed(0, own, flip(own, 0, lx))
            mid[y] = mixed(1, own, flip(own, 0, 2 * lx))
            to_core(y).start()

    if nz > 2:
        @when(gz < nz - 2)
        def _():
            halo_z(True).start()

        @when(gz > 1)
        def _():
            halo_z(False).start()

        @when(gz > 1)
        def _():
            halo_z(True).wait_recv()

        @when(gz < nz - 2)
        def _():
            halo_z(False).wait_recv()

    if not early:
        from_above()

    @when(gy > 0)
    def _():
        halo(True).wait_recv()

    @pl.loop(1 if early else 0, ly)
    def _(t):
        couple(ly - 1 - t)

    @pl.loop(0, leaf_ref.shape[0])
    def _(i):
        start = pl.multiple_of(i * ROWS, ROWS)
        along = [basis_of(pos_ref[d:d + 1, pl.ds(start, ROWS)]) for d in range(3)]
        last = jnp.concatenate(along[2], axis=0)
        for jx in range(PTS):
            tiles = [(along[0][jx] * along[1][jy]) * last for jy in range(PTS)]
            wts[i, jx * PTS * PTS:(jx + 1) * PTS * PTS] = jnp.concatenate(tiles, axis=0).astype(jnp.bfloat16)

    @pl.loop(0, ly)
    def _(t):
        y = ly - 1 - t
        for step in range(1, groups):
            back(y, step).wait_recv()
        for a in range(lx):
            for b in range(lz):
                parts = [home[g, y, a, b].astype(jnp.float32) for g in range(groups)]
                whole = [part[:per] for part in parts] + [part[per:] for part in parts]
                held[(a * ly + y) * lz + b] = jnp.concatenate(whole, axis=0).astype(jnp.bfloat16)

    @pl.loop(0, leaf_ref.shape[0] // 4)
    def _(k):
        for j in range(4):
            i = k * 4 + j
            values = jnp.dot(held[leaf_ref[i]], wts[i], preferred_element_type=jnp.float32).T
            live = lax.broadcasted_iota(jnp.int32, values.shape, 0) < count_ref[i]
            start = pl.multiple_of(i * ROWS, ROWS)
            out_ref[pl.ds(start, ROWS), :] = jnp.where(live, values, 0.0).astype(jnp.bfloat16)

    @pl.loop(0, ly)
    def _(t):
        for step in range(1, groups):
            forward(t, step).wait_send()
            back(t, step).wait_send()
        to_core(t).wait_send()

    @when(gy > 0)
    def _():
        halo(False).wait_send()

    @when(gy < ny - 1)
    def _():
        halo(True).wait_send()

    if nz > 2:
        @when(gz < nz - 2)
        def _():
            halo_z(True).wait_send()

        @when(gz > 1)
        def _():
            halo_z(False).wait_send()


def local(sizes, coefficients, level_weights, coupling, positions, block_leaf, block_count):
    nx, ny, nz = sizes
    lx, ly, lz, cheb, cols = coefficients.shape
    groups = 2 * nx
    rows = cols // groups
    bf = jnp.bfloat16
    plane = (nx * lx, 2 * lz, rows, cheb)
    dma = pltpu.SemaphoreType.DMA
    anywhere = pl.BlockSpec(memory_space=pl.ANY)
    vmem = pl.BlockSpec(memory_space=pltpu.VMEM)
    smem = pl.BlockSpec(memory_space=pltpu.SMEM)
    return pl.pallas_call(
        functools.partial(grid_kernel, sizes),
        out_shape=jax.ShapeDtypeStruct((positions.shape[1], cols), bf),
        in_specs=[smem, smem, vmem, vmem, anywhere, anywhere],
        out_specs=vmem,
        scratch_shapes=[
            pltpu.VMEM(level_weights.shape, bf),
            pltpu.VMEM(coupling.shape, bf),
            pltpu.VMEM((groups, ly, lx, lz, rows, cheb), bf),
            pltpu.VMEM((ly,) + plane, bf),
            pltpu.VMEM((ly,) + plane, bf),
            pltpu.VMEM((ly,) + plane, bf),
            pltpu.VMEM((ly + 2, nx * lx + 2, 2 * lz + 2, rows, cheb), bf),
            pltpu.VMEM((ly,) + plane, bf),
            pltpu.VMEM((groups, ly, lx, lz, rows, cheb), bf),
            pltpu.VMEM((lx * ly * lz, cols, cheb), bf),
            pltpu.VMEM((block_leaf.shape[0], cheb, ROWS), bf),
            dma((4,)), dma,
            dma((groups, ly)), dma((groups, ly)),
            dma((ly,)), dma((ly,)),
            dma((2,)), dma((2,)), dma((2,)), dma((2,)),
            dma((groups, ly)), dma((groups, ly)),
        ],
        compiler_params=pltpu.CompilerParams(
            collective_id=0, has_side_effects=True, vmem_limit_bytes=58 << 20
        ),
    )(block_leaf, block_count, coefficients, positions, level_weights, coupling)


def solution(mesh):
    sizes = (mesh.shape["gx"], mesh.shape["gy"], mesh.shape["gz"])
    placed = (
        P("gx", "gy", "gz", None, None),
        P(),
        P(),
        P(None, ("gx", "gy", "gz")),
        P(("gx", "gy", "gz")),
        P(("gx", "gy", "gz")),
    )
    return jax.shard_map(
        functools.partial(local, sizes), mesh=mesh, in_specs=placed,
        out_specs=P(("gx", "gy", "gz"), None), check_vma=False,
    )
```

```python
import functools
import math

import jax
import jax.numpy as jnp
from jax import lax
from jax.experimental import pallas as pl
from jax.experimental.pallas import tpu as pltpu
from jax.sharding import PartitionSpec as P

PTS = 8
ROWS = 128
MESH = pl.DeviceIdType.MESH
NT = (((1,), (1,)), ((), ()))


def flat(value):
    return value.reshape(-1, value.shape[-1])


def basis_of(coords):
    nodes = [math.cos(math.pi * (2 * j + 1) / (2 * PTS)) for j in range(PTS)]
    diffs = [coords - jnp.float32(node) for node in nodes]
    basis = []
    for j in range(PTS):
        scale = 1.0
        term = None
        for m in range(PTS):
            if m != j:
                scale *= nodes[j] - nodes[m]
                term = diffs[m] if term is None else term * diffs[m]
        basis.append(term * jnp.float32(1.0 / scale))
    return basis


def grid_kernel(sizes, leaf_ref, count_ref, x_ref, pos_ref, w_hbm, k_hbm, out_ref,
                w_ref, k_ref, src, xin, mid, got, pad, res, home, held, wts, part,
                w_sem, k_sem, fs_sem, fr_sem, ms_sem, mr_sem, hs_sem, hr_sem, zs_sem, zr_sem, bs_sem, br_sem):
    nx, ny, nz = sizes
    lx, ly, lz = x_ref.shape[:3]
    groups = 2 * nx
    per = x_ref.shape[-1] // 2 // groups
    gx, gy, gz = lax.axis_index("gx"), lax.axis_index("gy"), lax.axis_index("gz")
    bit = lax.rem(gz, 2)
    base = gz - bit
    me = gx * 2 + bit
    wide_x, wide_z = nx * lx, 2 * lz
    order = sorted(range(1, groups), key=lambda step: abs(step - groups // 2))

    def peer(step):
        other = lax.rem(me + step, groups)
        return other, lax.div(other, 2), lax.rem(other, 2)

    def when(cond):
        return pl.when(cond)

    for level in range(4):
        pltpu.make_async_copy(w_hbm.at[level], w_ref.at[level], w_sem.at[level]).start()
    pltpu.make_async_copy(k_hbm, k_ref, k_sem).start()

    barrier = pltpu.get_barrier_semaphore()
    for step in range(1, groups):
        _, px, pz = peer(step)
        pl.semaphore_signal(barrier, inc=1, device_id=(px, gy, base + pz), device_id_type=MESH)

    @when(gy > 0)
    def _():
        pl.semaphore_signal(barrier, inc=1, device_id=(gx, gy - 1, gz), device_id_type=MESH)

    @when(gy < ny - 1)
    def _():
        pl.semaphore_signal(barrier, inc=1, device_id=(gx, gy + 1, gz), device_id_type=MESH)

    if nz > 2:
        @when(gz > 1)
        def _():
            pl.semaphore_signal(barrier, inc=1, device_id=(gx, gy, gz - 2), device_id_type=MESH)

        @when(gz < nz - 2)
        def _():
            pl.semaphore_signal(barrier, inc=1, device_id=(gx, gy, gz + 2), device_id_type=MESH)

    def turn(t):
        y = lax.rem(ly - t, ly)
        for a in range(lx):
            for b in range(lz):
                block = x_ref[a, y, b].astype(jnp.float32).T
                half = block.shape[0] // 2
                for g in range(groups):
                    both = jnp.concatenate(
                        [block[g * per:(g + 1) * per], block[half + g * per:half + (g + 1) * per]], axis=0
                    )
                    src[g, y, a, b] = both.astype(jnp.bfloat16)
        xin[y, pl.ds(gx * lx, lx), pl.ds(bit * lz, lz)] = src[me, y]

    def forward(t, step):
        y = lax.rem(ly - t, ly)
        other, px, pz = peer(step)
        return pltpu.make_async_remote_copy(
            src_ref=src.at[other, y],
            dst_ref=xin.at[y, pl.ds(gx * lx, lx), pl.ds(bit * lz, lz)],
            send_sem=fs_sem.at[step, y],
            recv_sem=fr_sem.at[step, y],
            device_id=(px, gy, base + pz),
            device_id_type=MESH,
        )

    turn(0)
    def one(cond):
        return jnp.where(cond, 1, 0).astype(jnp.int32)

    peers = groups - 1 + one(gy > 0) + one(gy < ny - 1)
    if nz > 2:
        peers = peers + one(gz > 1) + one(gz < nz - 2)
    pl.semaphore_wait(barrier, peers)

    @pl.loop(0, ly)
    def _(t):
        @when(t > 0)
        def _():
            turn(t)
        for step in order:
            forward(t, step).start()

    pad[:, 0] = jnp.zeros_like(pad[:, 0])
    pad[:, wide_x + 1] = jnp.zeros_like(pad[:, 0])

    def no_plane(z):
        for y in range(1, ly + 1):
            pad[y, 1:wide_x + 1, z] = jnp.zeros_like(pad[0, 1:wide_x + 1, 0])

    if nz > 2:
        when(gz < 2)(lambda: no_plane(0))
        when(gz >= nz - 2)(lambda: no_plane(wide_z + 1))
    else:
        no_plane(0)
        no_plane(wide_z + 1)

    @when(gy == 0)
    def _():
        pad[0, 1:wide_x + 1] = jnp.zeros_like(pad[0, 1:wide_x + 1])

    @when(gy == ny - 1)
    def _():
        pad[ly + 1, 1:wide_x + 1] = jnp.zeros_like(pad[0, 1:wide_x + 1])

    def mixed(level, own, other):
        shape = own.shape
        a, b = flat(own), flat(other)
        dot = functools.partial(lax.dot_general, dimension_numbers=NT, preferred_element_type=jnp.float32)
        straight = dot(a, w_ref[level, 0, 0]) + dot(b, w_ref[level, 1, 0])
        cross = dot(a, w_ref[level, 0, 1]) + dot(b, w_ref[level, 1, 1])
        straight = straight.reshape(-1, 2, per, shape[-1])
        cross = cross.reshape(-1, 2, per, shape[-1])
        real = straight[:, 0] - cross[:, 1]
        imag = straight[:, 1] + cross[:, 0]
        return jnp.stack([real, imag], axis=1).reshape(shape).astype(jnp.bfloat16)

    def flip(value, dim, width):
        pieces = []
        for at in range(0, value.shape[dim], 2 * width):
            pieces.append(lax.slice_in_dim(value, at + width, at + 2 * width, axis=dim))
            pieces.append(lax.slice_in_dim(value, at, at + width, axis=dim))
        return jnp.concatenate(pieces, axis=dim)

    def to_core(y):
        return pltpu.make_async_remote_copy(
            src_ref=mid.at[y], dst_ref=got.at[y], send_sem=ms_sem.at[y], recv_sem=mr_sem.at[y],
            device_id=(gx, gy + 1 - 2 * lax.rem(gy, 2), gz), device_id_type=MESH,
        )

    inner = (pl.ds(1, wide_x), pl.ds(1, wide_z))

    def halo(up):
        return pltpu.make_async_remote_copy(
            src_ref=pad.at[(ly if up else 1,) + inner],
            dst_ref=pad.at[(0 if up else ly + 1,) + inner],
            send_sem=hs_sem.at[int(up)], recv_sem=hr_sem.at[int(up)],
            device_id=(gx, gy + 1 if up else gy - 1, gz), device_id_type=MESH,
        )

    def halo_z(up):
        rows = pl.ds(1, ly), pl.ds(1, wide_x)
        return pltpu.make_async_remote_copy(
            src_ref=pad.at[rows + (wide_z if up else 1,)],
            dst_ref=pad.at[rows + (0 if up else wide_z + 1,)],
            send_sem=zs_sem.at[int(up)], recv_sem=zr_sem.at[int(up)],
            device_id=(gx, gy, gz + 2 if up else gz - 2), device_id_type=MESH,
        )

    for level in range(4):
        pltpu.make_async_copy(w_hbm.at[level], w_ref.at[level], w_sem.at[level]).wait()

    def back(y, step):
        other, px, pz = peer(step)
        return pltpu.make_async_remote_copy(
            src_ref=res.at[y, pl.ds(px * lx, lx), pl.ds(pz * lz, lz)],
            dst_ref=home.at[me, y],
            send_sem=bs_sem.at[step, y], recv_sem=br_sem.at[step, y],
            device_id=(px, gy, base + pz), device_id_type=MESH,
        )

    def terms(y, total, dirs):
        xs, zs = pl.ds(1, wide_x), pl.ds(1, wide_z)
        places = (
            (y + 1, pl.ds(0, wide_x), zs), (y + 1, pl.ds(2, wide_x), zs),
            (y, xs, zs), (y + 2, xs, zs),
            (y + 1, xs, pl.ds(0, wide_z)), (y + 1, xs, pl.ds(2, wide_z)),
        )
        if total is None:
            total = flat(pad[y + 1, xs, zs]).astype(jnp.float32)
        for d in dirs:
            total = total + lax.dot_general(flat(pad[places[d]]), k_ref[d], NT, preferred_element_type=jnp.float32)
        return total

    def couple(y, total=None, dirs=range(6)):
        res[y] = terms(y, total, dirs).astype(jnp.bfloat16).reshape(res.shape[1:])
        for step in order:
            back(y, step).start()
        home[me, y] = res[y, pl.ds(gx * lx, lx), pl.ds(bit * lz, lz)]

    def from_above():
        pltpu.make_async_copy(k_hbm, k_ref, k_sem).wait()

        @when(gy < ny - 1)
        def _():
            halo(False).wait_recv()

    def from_below():
        @when(gy > 0)
        def _():
            halo(True).wait_recv()

    early = nz == 2 and ly == 4

    @pl.loop(0, ly + 1)
    def _(t):
        @when(t > 0)
        def _():
            y = lax.rem(ly + 1 - t, ly)
            to_core(y).wait_recv()
            own = mixed(2, mid[y], got[y])
            pad[y + 1, 1:wide_x + 1, 1:wide_z + 1] = mixed(3, own, flip(own, 1, lz))

            @when(jnp.logical_and(y == 0, gy > 0))
            def _():
                halo(False).start()

            @when(jnp.logical_and(y == ly - 1, gy < ny - 1))
            def _():
                halo(True).start()

        if early:
            @when(t == ly - 1)
            def _():
                from_above()
                couple(ly - 1)
                part[0] = terms(2, None, (0, 1, 3, 4, 5))
                from_below()
                part[1] = terms(0, None, (0, 1, 2, 4, 5))

        @when(t < ly)
        def _():
            y = lax.rem(ly - t, ly)
            for step in range(1, groups):
                forward(t, step).wait_recv()
            own = xin[y]
            own = mixed(0, own, flip(own, 0, lx))
            mid[y] = mixed(1, own, flip(own, 0, 2 * lx))
            to_core(y).start()

    if nz > 2:
        @when(gz < nz - 2)
        def _():
            halo_z(True).start()

        @when(gz > 1)
        def _():
            halo_z(False).start()

        @when(gz > 1)
        def _():
            halo_z(True).wait_recv()

        @when(gz < nz - 2)
        def _():
            halo_z(False).wait_recv()

    if early:
        couple(2, part[0], (2,))
        couple(0, part[1], (3,))
        couple(1)
    else:
        from_above()
        from_below()

        @pl.loop(0, ly)
        def _(t):
            couple(ly - 1 - t)

    @pl.loop(0, leaf_ref.shape[0])
    def _(i):
        start = pl.multiple_of(i * ROWS, ROWS)
        along = [basis_of(pos_ref[d:d + 1, pl.ds(start, ROWS)]) for d in range(3)]
        last = jnp.concatenate(along[2], axis=0)
        for jx in range(PTS):
            tiles = [(along[0][jx] * along[1][jy]) * last for jy in range(PTS)]
            wts[i, jx * PTS * PTS:(jx + 1) * PTS * PTS] = jnp.concatenate(tiles, axis=0).astype(jnp.bfloat16)

    @pl.loop(0, ly)
    def _(t):
        y = ly - 1 - t
        if early:
            late = lax.div(t, 2)
            y = late * (t - 2) + (1 - late) * y
        for step in range(1, groups):
            back(y, step).wait_recv()
        for a in range(lx):
            for b in range(lz):
                parts = [home[g, y, a, b].astype(jnp.float32) for g in range(groups)]
                whole = [part[:per] for part in parts] + [part[per:] for part in parts]
                held[(a * ly + y) * lz + b] = jnp.concatenate(whole, axis=0).astype(jnp.bfloat16)

    @pl.loop(0, leaf_ref.shape[0] // 4)
    def _(k):
        for j in range(4):
            i = k * 4 + j
            values = jnp.dot(held[leaf_ref[i]], wts[i], preferred_element_type=jnp.float32).T
            live = lax.broadcasted_iota(jnp.int32, values.shape, 0) < count_ref[i]
            start = pl.multiple_of(i * ROWS, ROWS)
            out_ref[pl.ds(start, ROWS), :] = jnp.where(live, values, 0.0).astype(jnp.bfloat16)

    @pl.loop(0, ly)
    def _(t):
        for step in range(1, groups):
            forward(t, step).wait_send()
            back(t, step).wait_send()
        to_core(t).wait_send()

    @when(gy > 0)
    def _():
        halo(False).wait_send()

    @when(gy < ny - 1)
    def _():
        halo(True).wait_send()

    if nz > 2:
        @when(gz < nz - 2)
        def _():
            halo_z(True).wait_send()

        @when(gz > 1)
        def _():
            halo_z(False).wait_send()


def local(sizes, coefficients, level_weights, coupling, positions, block_leaf, block_count):
    nx, ny, nz = sizes
    lx, ly, lz, cheb, cols = coefficients.shape
    groups = 2 * nx
    rows = cols // groups
    bf = jnp.bfloat16
    plane = (nx * lx, 2 * lz, rows, cheb)
    dma = pltpu.SemaphoreType.DMA
    anywhere = pl.BlockSpec(memory_space=pl.ANY)
    vmem = pl.BlockSpec(memory_space=pltpu.VMEM)
    smem = pl.BlockSpec(memory_space=pltpu.SMEM)
    return pl.pallas_call(
        functools.partial(grid_kernel, sizes),
        out_shape=jax.ShapeDtypeStruct((positions.shape[1], cols), bf),
        in_specs=[smem, smem, vmem, vmem, anywhere, anywhere],
        out_specs=vmem,
        scratch_shapes=[
            pltpu.VMEM(level_weights.shape, bf),
            pltpu.VMEM(coupling.shape, bf),
            pltpu.VMEM((groups, ly, lx, lz, rows, cheb), bf),
            pltpu.VMEM((ly,) + plane, bf),
            pltpu.VMEM((ly,) + plane, bf),
            pltpu.VMEM((ly,) + plane, bf),
            pltpu.VMEM((ly + 2, nx * lx + 2, 2 * lz + 2, rows, cheb), bf),
            pltpu.VMEM((ly,) + plane, bf),
            pltpu.VMEM((groups, ly, lx, lz, rows, cheb), bf),
            pltpu.VMEM((lx * ly * lz, cols, cheb), bf),
            pltpu.VMEM((block_leaf.shape[0], cheb, ROWS), bf),
            pltpu.VMEM((2, nx * lx * 2 * lz * rows, cheb), jnp.float32),
            dma((4,)), dma,
            dma((groups, ly)), dma((groups, ly)),
            dma((ly,)), dma((ly,)),
            dma((2,)), dma((2,)), dma((2,)), dma((2,)),
            dma((groups, ly)), dma((groups, ly)),
        ],
        compiler_params=pltpu.CompilerParams(
            collective_id=0, has_side_effects=True, vmem_limit_bytes=58 << 20
        ),
    )(block_leaf, block_count, coefficients, positions, level_weights, coupling)


def solution(mesh):
    sizes = (mesh.shape["gx"], mesh.shape["gy"], mesh.shape["gz"])
    placed = (
        P("gx", "gy", "gz", None, None),
        P(),
        P(),
        P(None, ("gx", "gy", "gz")),
        P(("gx", "gy", "gz")),
        P(("gx", "gy", "gz")),
    )
    return jax.shard_map(
        functools.partial(local, sizes), mesh=mesh, in_specs=placed,
        out_specs=P(("gx", "gy", "gz"), None), check_vma=False,
    )
```
